32 devices in a mesh: region: 4 (over z), row: 8 (over y, x, core).
Axes of the slice: x: 2, y: 2, z: 4, core: 2. Of those that a mesh axis runs over, the one named last changes fastest.
Arguments:
- state0: float32 [32, 16384], P(None, ('region', 'row')), may hold values from -6 to 6
- drive: bfloat16 [32, 16384], P(None, ('region', 'row')), may hold values from -6 to 6
- cotangent: float32 [32, 16384], P(None, ('region', 'row')), may hold values from -6 to 6
- excitatory: int32 [16384], P(('region', 'row')), may hold values 0 or 1
- tile_vals: bfloat16 [128, 24, 128, 128], P(('region', 'row')), may hold values from 0.0039978027 to 0.039794922
- tile_cols: int32 [128, 24], P(('region', 'row')), may hold values from 0 to 39
- tile_count: int32 [128], P(('region', 'row')), may hold values from 1 to 24, as said below
- boundary_rows: int32 [4, 8, 4, 32], P('region', 'row'), may hold values from 0 to 511, as said below
- u_factor: bfloat16 [32, 16384], P(None, ('region', 'row')), may hold values from -1 to 1
- v_factor: bfloat16 [32, 16384], P(None, ('region', 'row')), may hold values from -0.046875 to 0.046875
Outputs:
- final_state: float32 [32, 16384], P(None, ('region', 'row'))
- grad_u: float32 [32, 16384], P(None, ('region', 'row'))
- grad_v: float32 [32, 16384], P(None, ('region', 'row'))
The draws below stay inside these ranges and needn't reach their ends.
Inputs may be any that keep to these rules, and one draw needn't show every extreme that they name: tile_count[q] tiles of row tile q are live; its tiles j >= tile_count[q] take no part; the most, 24, is reached in every draw. `boundary_rows`: the 32 rows of one list are distinct. tile_cols[q, j] numbers a tile of 128 extended columns of the group of row tile q.
All inputs are finite; a program needn't handle non-finite values. No bound on the sum of `excitatory` on one device may be relied on, other than what follows from the above.
Results may differ from the reference program's by a relative error of at most 0.0055.
Values may be sent and summed in bfloat16 or wider, within the bound.
A program may use at most 64 MiB of HBM per device.

```python
import math
import jax
import jax.numpy as jnp
from jax import lax

BATCH = 32
ROWS_DEV = 512
KMAX = 24
BOUND = 128
RANK = 32
STEPS = 4
NEURONS = 16384
ROWTILES = 128
REGION_TILES = 32
COLT = 40
BSRC = 32
GROUPS = 4
ROW_DEVS = 8
N_REGION = 4
N_ROW = 8


def draw_tile_count(key, part):
    key_level, key_jitter, key_peak = jax.random.split(key, 3)
    levels = jax.random.randint(key_level, (ROWTILES // REGION_TILES,), KMAX // 4, KMAX + 1)
    jitter_width = KMAX // 8
    jitter = jax.random.randint(key_jitter, (ROWTILES,), -jitter_width, jitter_width + 1)
    counts = jnp.clip(jnp.repeat(levels, REGION_TILES) + jitter, 1, KMAX)
    peak_row = jax.random.randint(key_peak, (), 0, ROWTILES)
    return counts.at[peak_row].set(KMAX).astype(jnp.int32)


def draw_boundary_rows(key, part):
    list_count = GROUPS * ROW_DEVS * GROUPS
    keys_all = jax.random.split(key, list_count)
    chosen = jax.vmap(lambda one_key: jax.random.permutation(one_key, ROWS_DEV)[:BSRC])(keys_all)
    return chosen.reshape(GROUPS, ROW_DEVS, GROUPS, BSRC).astype(jnp.int32)


def touch_ends(values, own_key, smallest, high):
    index_at = [jax.random.randint(jax.random.fold_in(own_key, axis), (), 0, length) for axis, length in enumerate(values.shape)]
    main_axis = values.shape.index(max(values.shape))
    beside = index_at[:main_axis] + [(index_at[main_axis] + 1) % values.shape[main_axis]] + index_at[main_axis + 1:]
    return values.at[tuple(index_at)].set(smallest).at[tuple(beside)].set(high)


def block_levels(key, extent, pieces, least, top_value):
    factor_of, own = 1.0, jax.random.fold_in(key, 6)
    for axis_at, shards_of in pieces:
        heights = jnp.exp(jax.random.uniform(jax.random.fold_in(own, axis_at), (shards_of,), jnp.float32, least / len(pieces), top_value / len(pieces)))
        factor_of = factor_of * jnp.repeat(heights, extent[axis_at] // shards_of).reshape([-1 if axis == axis_at else 1 for axis in range(len(extent))])
    return factor_of


def bell_draw(own_key, shape, scale, reach, shards=(), kind=jnp.bfloat16):
    drawn = scale * jax.random.normal(own_key, shape, jnp.float32)
    if shards:
        drawn = drawn * block_levels(own_key, shape, shards, -0.22, 0.18)
    return jnp.clip(drawn, -reach, reach).astype(kind)


def setup_inputs(seed: int = 0) -> dict:
    key_list = jax.random.split(jax.random.key(seed), 11)
    return {
        "state0": bell_draw(key_list[0], (BATCH, NEURONS), 1.0, 6.0, ((1, 32),), jnp.float32),
        "drive": bell_draw(key_list[1], (BATCH, NEURONS), 1.0, 6.0, ((1, 32),)),
        "cotangent": bell_draw(key_list[2], (BATCH, NEURONS), 1.0, 6.0, ((1, 32),), jnp.float32),
        "excitatory": touch_ends((jax.random.randint(key_list[3], (NEURONS,), 0, 2) < 1).astype(jnp.int32), jax.random.fold_in(key_list[3], 1), 0, 1),
        "tile_vals": jnp.clip(jnp.exp(math.log(0.039794922) - 2.2979944 * jax.random.uniform(key_list[4], (ROWTILES, KMAX, 128, 128), jnp.float32) ** block_levels(key_list[4], (ROWTILES, KMAX, 128, 128), ((0, 32),), -0.2, 0.2)), 0.0039978027, 0.039794922).astype(jnp.bfloat16),
        "tile_cols": touch_ends(jax.random.randint(key_list[5], (ROWTILES, KMAX), 0, COLT), jax.random.fold_in(key_list[5], 1), 0, COLT - 1).astype(jnp.int32),
        "tile_count": draw_tile_count(jax.random.fold_in(key_list[10], 71), 0),
        "boundary_rows": draw_boundary_rows(jax.random.fold_in(key_list[10], 71), 0),
        "u_factor": bell_draw(key_list[8], (RANK, NEURONS), RANK ** -0.5, 1.0, ((1, 32),)),
        "v_factor": bell_draw(key_list[9], (RANK, NEURONS), NEURONS ** -0.5, 0.046875, ((1, 32),)),
    }


leak = 0.5


def reference(state0, drive, cotangent, excitatory, tile_vals, tile_cols, tile_count, boundary_rows, u_factor, v_factor):
    batch_rows = state0.shape[0]
    groups = N_REGION
    lanes = N_ROW
    region_tiles = ROWTILES // groups
    dev_tiles = ROWS_DEV // 128
    per_lane = (ROWS_DEV + BOUND) // 128
    col_tiles = lanes * per_lane
    polarity = (2 * excitatory - 1).astype(jnp.float32)
    source = jnp.arange(groups, dtype=jnp.int32)[:, None, None, None]
    lane_ids = jnp.arange(lanes, dtype=jnp.int32)[None, :, None, None]
    global_rows = (source * lanes + lane_ids) * ROWS_DEV + boundary_rows
    border_cols = jnp.transpose(global_rows, (2, 1, 0, 3)).reshape(groups, lanes, BOUND).astype(jnp.int32)
    live_all = jnp.arange(KMAX, dtype=jnp.int32)[None, :] < tile_count[:, None]
    live_group = live_all.reshape(groups, region_tiles, KMAX)
    tiles_group = tile_vals.reshape(groups, region_tiles, KMAX, 128, 128)
    cols_group = tile_cols.reshape(groups, region_tiles, KMAX)
    device_of = jnp.broadcast_to((jnp.arange(region_tiles, dtype=jnp.int32) // dev_tiles)[:, None], (region_tiles, KMAX))

    def forward_region(packed):
        ext_cols, tiles_one, cols_one, live_one = packed
        blocks = ext_cols[:, cols_one, :].astype(jnp.float32)
        blocks = jnp.where(live_one[None, :, :, None], blocks, 0.0)
        result = jnp.einsum("brjk,rjik->bri", blocks, tiles_one.astype(jnp.float32))
        return result.reshape(batch_rows, region_tiles * 128)

    def adjoint_region(packed):
        scaled_one, tiles_one, cols_one, live_one = packed
        spread = jnp.einsum("bri,rjik->brjk", scaled_one.astype(jnp.float32), tiles_one.astype(jnp.float32))
        spread = jnp.where(live_one[None, :, :, None], spread, 0.0)
        terms = jnp.zeros((lanes, col_tiles, batch_rows, 128), jnp.float32)
        terms = terms.at[device_of, cols_one].add(jnp.transpose(spread, (1, 2, 0, 3)))
        rounded = lax.optimization_barrier(terms.astype(jnp.bfloat16)).astype(jnp.float32)
        summed = jnp.sum(rounded, axis=0)
        summed = jnp.transpose(summed, (1, 0, 2)).reshape(batch_rows, lanes, per_lane * 128)
        return summed[:, :, :ROWS_DEV], summed[:, :, ROWS_DEV:]

    state = state0
    saved = []
    for moment in range(STEPS):
        rates = jnp.tanh(state)
        signed = (polarity * rates).astype(jnp.bfloat16)
        extended = jnp.concatenate([signed.reshape(batch_rows, groups, lanes, ROWS_DEV), signed[:, border_cols]], axis=3)
        ext_by_group = jnp.transpose(extended.reshape(batch_rows, groups, col_tiles, 128), (1, 0, 2, 3))
        synaptic = lax.map(forward_region, (ext_by_group, tiles_group, cols_group, live_group))
        synaptic = jnp.transpose(synaptic, (1, 0, 2)).reshape(batch_rows, NEURONS)
        latent = jnp.dot(signed, v_factor.T, preferred_element_type=jnp.float32).astype(jnp.bfloat16)
        lowrank = jnp.dot(latent, u_factor, preferred_element_type=jnp.float32)
        saved.append((rates, signed, latent))
        state = state + leak * (-state + synaptic + lowrank + drive.astype(jnp.float32))

    grad_u = jnp.zeros((RANK, NEURONS), jnp.float32)
    grad_v = jnp.zeros((RANK, NEURONS), jnp.float32)
    adjoint = cotangent
    for moment in reversed(range(STEPS)):
        rates, signed, latent = saved[moment]
        scaled = (leak * adjoint).astype(jnp.bfloat16)
        coeffs = jnp.dot(scaled, u_factor.T, preferred_element_type=jnp.float32).astype(jnp.bfloat16)
        scaled_group = jnp.transpose(scaled.reshape(batch_rows, groups, region_tiles, 128), (1, 0, 2, 3))
        own_all, border_all = lax.map(adjoint_region, (scaled_group, tiles_group, cols_group, live_group))
        own_flat = jnp.transpose(own_all, (1, 0, 2, 3)).reshape(batch_rows, NEURONS)
        border_flat = jnp.transpose(border_all, (1, 0, 2, 3)).reshape(batch_rows, groups * lanes * BOUND)
        through = own_flat.at[:, border_cols.reshape(-1)].add(border_flat)
        total_signed = through + jnp.dot(coeffs, v_factor, preferred_element_type=jnp.float32)
        grad_u = grad_u + jnp.dot(latent.T, scaled, preferred_element_type=jnp.float32)
        grad_v = grad_v + jnp.dot(coeffs.T, signed, preferred_element_type=jnp.float32)
        adjoint = (1.0 - leak) * adjoint + (1.0 - rates * rates) * polarity * total_signed
    return (state, grad_u, grad_v)
```

```python
import functools

import jax
import jax.numpy as jnp
from jax import lax
from jax.experimental import pallas as pl
from jax.experimental.pallas import tpu as pltpu
from jax.sharding import PartitionSpec as P

STEPS = 4
LEAK = 0.5
F32 = jnp.float32
BF16 = jnp.bfloat16
MESH = pl.DeviceIdType.MESH
NT = (((1,), (1,)), ((), ()))
NN = (((1,), (0,)), ((), ()))


def dense_kernel(lanes, per_lane, cols_ref, count_ref, vals_ref, own_ref, border_ref, acc):
    q = pl.program_id(0)
    own_tiles = per_lane - 1
    acc[...] = jnp.zeros_like(acc)

    def add(j, carry):
        c = cols_ref[q, j]
        acc[c] = acc[c] + vals_ref[0, j].astype(F32)
        return carry

    lax.fori_loop(0, count_ref[q], add, 0)
    for lane in range(lanes):
        for i in range(own_tiles):
            own_ref[lane, :, i * 128 : (i + 1) * 128] = acc[lane * per_lane + i].astype(BF16)
        border_ref[:, lane * 128 : (lane + 1) * 128] = acc[lane * per_lane + own_tiles].astype(BF16)


def densify(tile_vals, tile_cols, tile_count, lanes, own_rows):
    row_tiles, kmax = tile_vals.shape[:2]
    per_lane = own_rows // 128 + 1
    return pl.pallas_call(
        functools.partial(dense_kernel, lanes, per_lane),
        out_shape=(
            jax.ShapeDtypeStruct((lanes, own_rows, own_rows), BF16),
            jax.ShapeDtypeStruct((own_rows, lanes * 128), BF16),
        ),
        grid_spec=pltpu.PrefetchScalarGridSpec(
            num_scalar_prefetch=2,
            grid=(row_tiles,),
            in_specs=[pl.BlockSpec((1, kmax, 128, 128), lambda q, *_: (q, 0, 0, 0))],
            out_specs=[
                pl.BlockSpec((lanes, 128, own_rows), lambda q, *_: (0, q, 0)),
                pl.BlockSpec((128, lanes * 128), lambda q, *_: (q, 0)),
            ],
            scratch_shapes=[pltpu.VMEM((lanes * per_lane, 128, 128), F32)],
        ),
        compiler_params=pltpu.CompilerParams(vmem_limit_bytes=48 * 1024 * 1024),
    )(tile_cols, tile_count, tile_vals)


def fold(x, rank):
    shift = 64
    while shift >= rank:
        x = x + pltpu.roll(x, shift, 1)
        shift //= 2
    return x


def round_trip(x):
    return x.astype(BF16).astype(F32)


def step_kernel(
    groups,
    lanes,
    bsrc,
    state_ref,
    drive_ref,
    cot_ref,
    exc_ref,
    own_hbm,
    border_hbm,
    rows_ref,
    u_ref,
    v_ref,
    final_ref,
    gu_ref,
    gv_ref,
    a_own,
    a_border,
    pick,
    ext,
    zsend,
    zbuf,
    bbuf,
    rsend,
    rbuf,
    azsend,
    azbuf,
    rates_sv,
    signed_sv,
    scaled_sv,
    lat_sv,
    coef_sv,
    adj_sv,
    state_sv,
    load_sem,
    ext_s,
    ext_r,
    z_s,
    z_r,
    b_s,
    b_r,
    r_s,
    r_r,
    az_s,
    az_r,
):
    g = lax.axis_index("region")
    w = lax.axis_index("row")
    batch, own = state_ref.shape
    rank = u_ref.shape[0]

    load_own = pltpu.make_async_copy(own_hbm, a_own, load_sem.at[0])
    load_border = pltpu.make_async_copy(border_hbm, a_border, load_sem.at[1])
    load_own.start()
    load_border.start()

    def row_peer(d):
        return lax.rem(w + d, lanes)

    def region_peer(d):
        return lax.rem(g + d, groups)

    barrier = pltpu.get_barrier_semaphore()

    def greet_row(d, carry):
        pl.semaphore_signal(barrier, inc=1, device_id=(g, row_peer(d)), device_id_type=MESH)
        return carry

    def greet_region(d, carry):
        pl.semaphore_signal(barrier, inc=1, device_id=(region_peer(d), w), device_id_type=MESH)
        return carry

    lax.fori_loop(1, lanes, greet_row, 0)
    lax.fori_loop(1, groups, greet_region, 0)

    lane = lax.broadcasted_iota(jnp.int32, (batch, 128), 1)

    def offset(s):
        return lax.rem(lane + (128 * bsrc - bsrc * s), 128)

    def is_border(s):
        return offset(s) < bsrc

    def is_low_border(s):
        return (offset(s) >= bsrc) & (offset(s) < 2 * bsrc)

    def is_high(s):
        return (offset(s) >= 2 * bsrc) & (offset(s) < 2 * bsrc + rank)

    def is_low(s):
        return (offset(s) >= 2 * bsrc + rank) & (offset(s) < 2 * bsrc + 2 * rank)

    def is_sum(s):
        return is_high(s) | is_low(s)

    def sum_tile(x):
        high = round_trip(x)
        return jnp.where(lane < rank, x, jnp.where(lane < 2 * rank, x - high, 0.0)).astype(BF16)

    polarity = (2 * exc_ref[...] - 1).astype(F32)
    u_all = jnp.concatenate([u_ref[...]] * (128 // rank), axis=0)
    v_cols = jnp.concatenate([v_ref[...].astype(F32)] * (128 // rank), axis=0).T
    sub = lax.broadcasted_iota(jnp.int32, (own, 128), 0)
    own_lane = lax.rem(
        lax.broadcasted_iota(jnp.int32, (own, 128), 1) + (128 * bsrc - bsrc * g), 128
    )
    for s in range(groups):
        hot = jnp.where(sub == rows_ref[s : s + 1, :], 1.0, 0.0)
        pick[:, s * 128 : (s + 1) * 128] = jnp.where(own_lane < 2 * bsrc, hot, v_cols).astype(BF16)

    def row_copy(kind, t, d, src, dst):
        send, recv = kind
        return pltpu.make_async_remote_copy(
            src_ref=src,
            dst_ref=dst,
            send_sem=send.at[t, d],
            recv_sem=recv.at[t, w],
            device_id=(g, row_peer(d)),
            device_id_type=MESH,
        )

    def region_copy(kind, t, d, src, dst):
        send, recv = kind
        return pltpu.make_async_remote_copy(
            src_ref=src,
            dst_ref=dst,
            send_sem=send.at[t, d],
            recv_sem=recv.at[t, g],
            device_id=(region_peer(d), w),
            device_id_type=MESH,
        )

    def arrive(recv, t, source, ref):
        pltpu.make_async_copy(ref, ref, recv.at[t, source]).wait()

    def each(low, high, body):
        def step(d, carry):
            body(d)
            return carry

        lax.fori_loop(low, high, step, 0)

    def forward_send(t, state):
        rates = jnp.tanh(state)
        signed = (polarity * rates).astype(BF16)
        rates_sv[t] = rates
        signed_sv[t] = signed
        message = lax.dot_general(signed, pick[...], NN, preferred_element_type=F32)
        mine_low = is_low(g)
        for s in range(groups):
            tile = message[:, s * 128 : (s + 1) * 128]
            zsend[t, s] = jnp.where(mine_low, tile - round_trip(tile), tile).astype(BF16)
        each(
            1,
            groups,
            lambda d: region_copy(
                (z_s, z_r), t, d, zsend.at[t, region_peer(d)], zbuf.at[t, g]
            ).start(),
        )
        ext[t, w] = signed
        each(
            1,
            lanes,
            lambda d: row_copy((ext_s, ext_r), t, d, ext.at[t, w], ext.at[t, w]).start(),
        )
        zbuf[t, g] = zsend[t, g]

    def forward_merge(t):
        each(1, groups, lambda d: arrive(z_r, t, region_peer(d), zbuf.at[t, region_peer(d)]))
        border = jnp.zeros((batch, 128), F32)
        latent = jnp.zeros((batch, 128), F32)
        for s in range(groups):
            tile = zbuf[t, s].astype(F32)
            border = jnp.where(is_border(s), tile, border)
            latent = latent + jnp.where(is_sum(s), tile, 0.0)
        bbuf[t, w, :, 0:128] = border.astype(BF16)
        bbuf[t, w, :, 128:256] = sum_tile(fold(latent, rank))
        each(
            1,
            lanes,
            lambda d: row_copy((b_s, b_r), t, d, bbuf.at[t, w], bbuf.at[t, w]).start(),
        )

    def forward_finish(t, state):
        def gather(d, total):
            peer = row_peer(d)
            arrive(ext_r, t, peer, ext.at[t, peer])
            return total + lax.dot_general(
                ext[t, peer], a_own[peer], NT, preferred_element_type=F32
            )

        total = lax.dot_general(ext[t, w], a_own[w], NT, preferred_element_type=F32)
        total = lax.fori_loop(1, lanes, gather, total)
        each(1, lanes, lambda d: arrive(b_r, t, row_peer(d), bbuf.at[t, row_peer(d)]))
        latent = jnp.zeros((batch, 128), F32)
        tiles = []
        for lane_at in range(lanes):
            tiles.append(bbuf[t, lane_at, :, 0:128])
            latent = latent + bbuf[t, lane_at, :, 128:256].astype(F32)
        total = total + lax.dot_general(
            jnp.concatenate(tiles, axis=1), a_border[...], NT, preferred_element_type=F32
        )
        latent = round_trip(fold(latent, rank))
        lat_sv[t * batch : (t + 1) * batch, :] = latent
        total = total + lax.dot_general(
            latent[:, :rank].astype(BF16), u_ref[...], NN, preferred_element_type=F32
        )
        return state + LEAK * (-state + total + drive_ref[...].astype(F32))

    def adjoint_send(t, adjoint):
        scaled = (LEAK * adjoint).astype(BF16)
        scaled_sv[t * batch : (t + 1) * batch, :] = scaled
        coeff = sum_tile(lax.dot_general(scaled, u_all, NT, preferred_element_type=F32))
        if t == 0:
            rbuf[t, w, :, own + 128 : own + 256] = coeff
            part = pl.ds(own + 128, 128)
            each(
                1,
                lanes,
                lambda d: row_copy(
                    (r_s, r_r), t, d, rbuf.at[t, w, :, part], rbuf.at[t, w, :, part]
                ).start(),
            )
            return
        border = lax.dot_general(scaled, a_border[...], NN, preferred_element_type=F32).astype(BF16)
        for lane_at in range(lanes):
            rsend[t, lane_at, :, own : own + 128] = border[:, lane_at * 128 : (lane_at + 1) * 128]
            rsend[t, lane_at, :, own + 128 : own + 256] = coeff

        def spread(peer):
            return lax.dot_general(scaled, a_own[peer], NN, preferred_element_type=F32).astype(BF16)

        def push(d):
            peer = row_peer(d)
            rsend[t, peer, :, 0:own] = spread(peer)
            row_copy((r_s, r_r), t, d, rsend.at[t, peer], rbuf.at[t, w]).start()

        each(1, lanes, push)
        rbuf[t, w, :, 0:own] = spread(w)
        rbuf[t, w, :, own : own + 256] = rsend[t, w, :, own : own + 256]

    def adjoint_merge(t):
        low = own + 128 if t == 0 else 0
        part = pl.ds(low, own + 256 - low)
        each(
            1,
            lanes,
            lambda d: arrive(r_r, t, row_peer(d), rbuf.at[t, row_peer(d), :, part]),
        )
        summed = rbuf[t, 0, :, part].astype(F32)
        for lane_at in range(1, lanes):
            summed = summed + rbuf[t, lane_at, :, part].astype(F32)
        coeff = fold(summed[:, own + 128 - low :], rank)
        coeff_low = coeff - round_trip(coeff)
        if t == 0:
            border = border_low = jnp.zeros((batch, 128), F32)
        else:
            border = summed[:, own : own + 128]
            border_low = pltpu.roll(border - round_trip(border), bsrc, 1)
        for s in range(groups):
            tile = jnp.where(
                is_border(s),
                border,
                jnp.where(is_low_border(s), border_low, jnp.where(is_high(s), coeff, coeff_low)),
            )
            azsend[t, s] = tile.astype(BF16)
        each(
            1,
            groups,
            lambda d: region_copy(
                (az_s, az_r), t, d, azsend.at[t, region_peer(d)], azbuf.at[t, g]
            ).start(),
        )
        azbuf[t, g] = azsend[t, g]
        return None if t == 0 else summed[:, :own]

    def adjoint_finish(t, through):
        each(1, groups, lambda d: arrive(az_r, t, region_peer(d), azbuf.at[t, region_peer(d)]))
        mine = is_sum(g)
        coeff = jnp.zeros((batch, 128), F32)
        for s in range(groups):
            coeff = coeff + jnp.where(mine, azbuf[t, s].astype(F32), 0.0)
        coeff = round_trip(fold(coeff, rank))
        coef_sv[t * batch : (t + 1) * batch, :] = coeff
        if t == 0:
            return None
        home = offset(g) < 2 * bsrc
        tiles = []
        for s in range(groups):
            rest = jnp.where(is_high(g), coeff, 0.0) if s == 0 else jnp.zeros_like(coeff)
            tiles.append(jnp.where(home, azbuf[t, s].astype(F32), rest).astype(BF16))
        return through + lax.dot_general(
            jnp.concatenate(tiles, axis=1), pick[...], NT, preferred_element_type=F32
        )

    def adjoint_step(t, adjoint, total):
        rates = rates_sv[t]
        return (1.0 - LEAK) * adjoint + (1.0 - rates * rates) * polarity * total

    pl.semaphore_wait(barrier, lanes + groups - 2)

    last = STEPS - 1
    state = state_ref[...]
    forward_send(0, state)
    forward_merge(0)
    load_own.wait()
    load_border.wait()
    state = forward_finish(0, state)

    forward_send(1, state)
    adjoint_send(last, cot_ref[...])
    forward_merge(1)
    state = forward_finish(1, state)

    forward_send(2, state)
    forward_merge(2)
    adj_sv[...] = adjoint_merge(last)
    state = forward_finish(2, state)

    rates_sv[last] = jnp.tanh(state)
    state_sv[...] = state
    adjoint = adjoint_step(last, cot_ref[...], adjoint_finish(last, adj_sv[...]))
    adjoint_send(2, adjoint)
    forward_send(last, state_sv[...])
    forward_merge(last)
    through = adjoint_merge(2)
    adjoint = adjoint_step(2, adjoint, adjoint_finish(2, through))
    adjoint_send(1, adjoint)
    final_ref[...] = forward_finish(last, state_sv[...])
    through = adjoint_merge(1)
    adjoint = adjoint_step(1, adjoint, adjoint_finish(1, through))
    adjoint_send(0, adjoint)
    lat = lat_sv[...].T[:rank].astype(BF16)
    gu_ref[...] = lax.dot_general(lat, scaled_sv[...], NN, preferred_element_type=F32)
    adjoint_merge(0)
    adjoint_finish(0, None)
    coef = coef_sv[...].T[:rank].astype(BF16)
    signed_all = jnp.concatenate([signed_sv[t] for t in range(STEPS)], axis=0)
    gv_ref[...] = lax.dot_general(coef, signed_all, NN, preferred_element_type=F32)

    for t in range(STEPS):
        each(
            1,
            groups,
            lambda d: region_copy(
                (z_s, z_r), t, d, zsend.at[t, region_peer(d)], zbuf.at[t, g]
            ).wait_send(),
        )
        each(
            1,
            groups,
            lambda d: region_copy(
                (az_s, az_r), t, d, azsend.at[t, region_peer(d)], azbuf.at[t, g]
            ).wait_send(),
        )

        def drain(d):
            row_copy((ext_s, ext_r), t, d, ext.at[t, w], ext.at[t, w]).wait_send()
            row_copy((b_s, b_r), t, d, bbuf.at[t, w], bbuf.at[t, w]).wait_send()
            if t == 0:
                part = pl.ds(own + 128, 128)
                row_copy(
                    (r_s, r_r), t, d, rbuf.at[t, w, :, part], rbuf.at[t, w, :, part]
                ).wait_send()
            else:
                row_copy((r_s, r_r), t, d, rsend.at[t, row_peer(d)], rbuf.at[t, w]).wait_send()

        each(1, lanes, drain)


def local(
    state0,
    drive,
    cotangent,
    excitatory,
    tile_vals,
    tile_cols,
    tile_count,
    boundary_rows,
    u_factor,
    v_factor,
):
    lanes = lax.axis_size("row")
    groups, bsrc = boundary_rows.shape[2:]
    batch, own = state0.shape
    rank = u_factor.shape[0]
    a_own, a_border = densify(tile_vals, tile_cols, tile_count, lanes, own)
    rows = jnp.tile(boundary_rows.reshape(groups, bsrc), (1, 128 // bsrc))
    vmem = pl.BlockSpec(memory_space=pltpu.VMEM)
    hbm = pl.BlockSpec(memory_space=pl.ANY)
    dma = pltpu.SemaphoreType.DMA
    out = jax.ShapeDtypeStruct((batch, own), F32)
    grad = jax.ShapeDtypeStruct((rank, own), F32)
    return pl.pallas_call(
        functools.partial(step_kernel, groups, lanes, bsrc),
        out_shape=(out, grad, grad),
        in_specs=[vmem, vmem, vmem, vmem, hbm, hbm, vmem, vmem, vmem],
        out_specs=(vmem, vmem, vmem),
        scratch_shapes=[
            pltpu.VMEM((lanes, own, own), BF16),
            pltpu.VMEM((own, lanes * 128), BF16),
            pltpu.VMEM((own, groups * 128), BF16),
            pltpu.VMEM((STEPS, lanes, batch, own), BF16),
            pltpu.VMEM((STEPS, groups, batch, 128), BF16),
            pltpu.VMEM((STEPS, groups, batch, 128), BF16),
            pltpu.VMEM((STEPS, lanes, batch, 256), BF16),
            pltpu.VMEM((STEPS, lanes, batch, own + 256), BF16),
            pltpu.VMEM((STEPS, lanes, batch, own + 256), BF16),
            pltpu.VMEM((STEPS, groups, batch, 128), BF16),
            pltpu.VMEM((STEPS, groups, batch, 128), BF16),
            pltpu.VMEM((STEPS, batch, own), F32),
            pltpu.VMEM((STEPS, batch, own), BF16),
            pltpu.VMEM((STEPS * batch, own), BF16),
            pltpu.VMEM((STEPS * batch, 128), F32),
            pltpu.VMEM((STEPS * batch, 128), F32),
            pltpu.VMEM((batch, own), F32),
            pltpu.VMEM((batch, own), F32),
            dma((2,)),
            dma((STEPS, lanes)),
            dma((STEPS, lanes)),
            dma((STEPS, groups)),
            dma((STEPS, groups)),
            dma((STEPS, lanes)),
            dma((STEPS, lanes)),
            dma((STEPS, lanes)),
            dma((STEPS, lanes)),
            dma((STEPS, groups)),
            dma((STEPS, groups)),
        ],
        compiler_params=pltpu.CompilerParams(
            collective_id=0, has_side_effects=True, vmem_limit_bytes=60 * 1024 * 1024
        ),
    )(
        state0,
        drive,
        cotangent,
        excitatory.reshape(1, own),
        a_own,
        a_border,
        rows,
        u_factor,
        v_factor,
    )


def solution(mesh):
    return jax.shard_map(
        local,
        mesh=mesh,
        in_specs=(
            P(None, ("region", "row")),
            P(None, ("region", "row")),
            P(None, ("region", "row")),
            P(("region", "row")),
            P(("region", "row"), None, None, None),
            P(("region", "row"), None),
            P(("region", "row")),
            P("region", "row", None, None),
            P(None, ("region", "row")),
            P(None, ("region", "row")),
        ),
        out_specs=(
            P(None, ("region", "row")),
            P(None, ("region", "row")),
            P(None, ("region", "row")),
        ),
        check_vma=False,
    )
```

```python
import functools

import jax
import jax.numpy as jnp
from jax import lax
from jax.experimental import pallas as pl
from jax.experimental.pallas import tpu as pltpu
from jax.sharding import PartitionSpec as P

STEPS = 4
LEAK = 0.5
F32 = jnp.float32
BF16 = jnp.bfloat16
MESH = pl.DeviceIdType.MESH
NT = (((1,), (1,)), ((), ()))
NN = (((1,), (0,)), ((), ()))


def dense_kernel(lanes, per_lane, cols_ref, count_ref, vals_ref, own_ref, border_ref, acc):
    q = pl.program_id(0)
    own_tiles = per_lane - 1
    acc[...] = jnp.zeros_like(acc)

    def add(j, carry):
        c = cols_ref[q, j]
        acc[c] = acc[c] + vals_ref[0, j].astype(F32)
        return carry

    lax.fori_loop(0, count_ref[q], add, 0)
    for lane in range(lanes):
        for i in range(own_tiles):
            own_ref[lane, :, i * 128 : (i + 1) * 128] = acc[lane * per_lane + i].astype(BF16)
        border_ref[:, lane * 128 : (lane + 1) * 128] = acc[lane * per_lane + own_tiles].astype(BF16)


def densify(tile_vals, tile_cols, tile_count, lanes, own_rows):
    row_tiles, kmax = tile_vals.shape[:2]
    per_lane = own_rows // 128 + 1
    return pl.pallas_call(
        functools.partial(dense_kernel, lanes, per_lane),
        out_shape=(
            jax.ShapeDtypeStruct((lanes, own_rows, own_rows), BF16),
            jax.ShapeDtypeStruct((own_rows, lanes * 128), BF16),
        ),
        grid_spec=pltpu.PrefetchScalarGridSpec(
            num_scalar_prefetch=2,
            grid=(row_tiles,),
            in_specs=[pl.BlockSpec((1, kmax, 128, 128), lambda q, *_: (q, 0, 0, 0))],
            out_specs=[
                pl.BlockSpec((lanes, 128, own_rows), lambda q, *_: (0, q, 0)),
                pl.BlockSpec((128, lanes * 128), lambda q, *_: (q, 0)),
            ],
            scratch_shapes=[pltpu.VMEM((lanes * per_lane, 128, 128), F32)],
        ),
        compiler_params=pltpu.CompilerParams(vmem_limit_bytes=48 * 1024 * 1024),
    )(tile_cols, tile_count, tile_vals)


def fold(x, rank):
    shift = 64
    while shift >= rank:
        x = x + pltpu.roll(x, shift, 1)
        shift //= 2
    return x


def round_trip(x):
    return x.astype(BF16).astype(F32)


def step_kernel(
    groups,
    lanes,
    bsrc,
    state_ref,
    drive_ref,
    cot_ref,
    exc_ref,
    own_hbm,
    border_hbm,
    rows_ref,
    u_ref,
    v_ref,
    final_ref,
    gu_ref,
    gv_ref,
    a_own,
    a_border,
    pick,
    ext,
    zsend,
    zbuf,
    bbuf,
    rsend,
    rbuf,
    azsend,
    azbuf,
    rates_sv,
    signed_sv,
    scaled_sv,
    lat_sv,
    coef_sv,
    adj_sv,
    state_sv,
    load_sem,
    ext_s,
    ext_r,
    z_s,
    z_r,
    b_s,
    b_r,
    r_s,
    r_r,
    az_s,
    az_r,
):
    g = lax.axis_index("region")
    w = lax.axis_index("row")
    batch, own = state_ref.shape
    rank = u_ref.shape[0]

    load_own = pltpu.make_async_copy(own_hbm, a_own, load_sem.at[0])
    load_border = pltpu.make_async_copy(border_hbm, a_border, load_sem.at[1])
    load_own.start()
    load_border.start()

    def row_peer(d):
        return lax.rem(w + d, lanes)

    def region_peer(d):
        return lax.rem(g + d, groups)

    barrier = pltpu.get_barrier_semaphore()

    def greet_row(d, carry):
        pl.semaphore_signal(barrier, inc=1, device_id=(g, row_peer(d)), device_id_type=MESH)
        return carry

    def greet_region(d, carry):
        pl.semaphore_signal(barrier, inc=1, device_id=(region_peer(d), w), device_id_type=MESH)
        return carry

    lax.fori_loop(1, lanes, greet_row, 0)
    lax.fori_loop(1, groups, greet_region, 0)

    lane = lax.broadcasted_iota(jnp.int32, (batch, 128), 1)

    def offset(s):
        return lax.rem(lane + (128 * bsrc - bsrc * s), 128)

    def is_border(s):
        return offset(s) < bsrc

    def is_low_border(s):
        return (offset(s) >= bsrc) & (offset(s) < 2 * bsrc)

    def is_high(s):
        return (offset(s) >= 2 * bsrc) & (offset(s) < 2 * bsrc + rank)

    def is_low(s):
        return (offset(s) >= 2 * bsrc + rank) & (offset(s) < 2 * bsrc + 2 * rank)

    def is_sum(s):
        return is_high(s) | is_low(s)

    def sum_tile(x):
        high = round_trip(x)
        return jnp.where(lane < rank, x, jnp.where(lane < 2 * rank, x - high, 0.0)).astype(BF16)

    polarity = (2 * exc_ref[...] - 1).astype(F32)
    u_all = jnp.concatenate([u_ref[...]] * (128 // rank), axis=0)
    v_cols = jnp.concatenate([v_ref[...].astype(F32)] * (128 // rank), axis=0).T
    sub = lax.broadcasted_iota(jnp.int32, (own, 128), 0)
    own_lane = lax.rem(
        lax.broadcasted_iota(jnp.int32, (own, 128), 1) + (128 * bsrc - bsrc * g), 128
    )
    rows = jnp.concatenate([rows_ref[...]] * (128 // bsrc), axis=1)
    for s in range(groups):
        hot = jnp.where(sub == rows[s : s + 1, :], 1.0, 0.0)
        pick[:, s * 128 : (s + 1) * 128] = jnp.where(own_lane < 2 * bsrc, hot, v_cols).astype(BF16)

    def row_copy(kind, t, d, src, dst):
        send, recv = kind
        return pltpu.make_async_remote_copy(
            src_ref=src,
            dst_ref=dst,
            send_sem=send.at[t, d],
            recv_sem=recv.at[t, w],
            device_id=(g, row_peer(d)),
            device_id_type=MESH,
        )

    def region_copy(kind, t, d, src, dst):
        send, recv = kind
        return pltpu.make_async_remote_copy(
            src_ref=src,
            dst_ref=dst,
            send_sem=send.at[t, d],
            recv_sem=recv.at[t, g],
            device_id=(region_peer(d), w),
            device_id_type=MESH,
        )

    def arrive(recv, t, source, ref):
        pltpu.make_async_copy(ref, ref, recv.at[t, source]).wait()

    def each(low, high, body):
        def step(d, carry):
            body(d)
            return carry

        lax.fori_loop(low, high, step, 0)

    def forward_send(t, state):
        rates = jnp.tanh(state)
        signed = (polarity * rates).astype(BF16)
        rates_sv[t] = rates
        signed_sv[t] = signed
        message = lax.dot_general(signed, pick[...], NN, preferred_element_type=F32)
        mine_low = is_low(g)
        for s in range(groups):
            tile = message[:, s * 128 : (s + 1) * 128]
            zsend[t, s] = jnp.where(mine_low, tile - round_trip(tile), tile).astype(BF16)
        each(
            1,
            groups,
            lambda d: region_copy(
                (z_s, z_r), t, d, zsend.at[t, region_peer(d)], zbuf.at[t, g]
            ).start(),
        )
        ext[t, w] = signed
        each(
            1,
            lanes,
            lambda d: row_copy((ext_s, ext_r), t, d, ext.at[t, w], ext.at[t, w]).start(),
        )
        zbuf[t, g] = zsend[t, g]

    def forward_merge(t):
        each(1, groups, lambda d: arrive(z_r, t, region_peer(d), zbuf.at[t, region_peer(d)]))
        border = jnp.zeros((batch, 128), F32)
        latent = jnp.zeros((batch, 128), F32)
        for s in range(groups):
            tile = zbuf[t, s].astype(F32)
            border = jnp.where(is_border(s), tile, border)
            latent = latent + jnp.where(is_sum(s), tile, 0.0)
        bbuf[t, w, :, 0:128] = border.astype(BF16)
        bbuf[t, w, :, 128:256] = sum_tile(fold(latent, rank))
        each(
            1,
            lanes,
            lambda d: row_copy((b_s, b_r), t, d, bbuf.at[t, w], bbuf.at[t, w]).start(),
        )

    def forward_finish(t, state):
        def gather(d, total):
            peer = row_peer(d)
            arrive(ext_r, t, peer, ext.at[t, peer])
            return total + lax.dot_general(
                ext[t, peer], a_own[peer], NT, preferred_element_type=F32
            )

        total = lax.dot_general(ext[t, w], a_own[w], NT, preferred_element_type=F32)
        total = lax.fori_loop(1, lanes, gather, total)
        each(1, lanes, lambda d: arrive(b_r, t, row_peer(d), bbuf.at[t, row_peer(d)]))
        latent = jnp.zeros((batch, 128), F32)
        tiles = []
        for lane_at in range(lanes):
            tiles.append(bbuf[t, lane_at, :, 0:128])
            latent = latent + bbuf[t, lane_at, :, 128:256].astype(F32)
        total = total + lax.dot_general(
            jnp.concatenate(tiles, axis=1), a_border[...], NT, preferred_element_type=F32
        )
        latent = round_trip(fold(latent, rank))
        lat_sv[t * batch : (t + 1) * batch, :] = latent
        total = total + lax.dot_general(
            latent[:, :rank].astype(BF16), u_ref[...], NN, preferred_element_type=F32
        )
        return state + LEAK * (-state + total + drive_ref[...].astype(F32))

    def adjoint_send(t, adjoint):
        scaled = (LEAK * adjoint).astype(BF16)
        scaled_sv[t * batch : (t + 1) * batch, :] = scaled
        coeff = sum_tile(lax.dot_general(scaled, u_all, NT, preferred_element_type=F32))
        if t == 0:
            rbuf[t, w, :, own + 128 : own + 256] = coeff
            part = pl.ds(own + 128, 128)
            each(
                1,
                lanes,
                lambda d: row_copy(
                    (r_s, r_r), t, d, rbuf.at[t, w, :, part], rbuf.at[t, w, :, part]
                ).start(),
            )
            return
        border = lax.dot_general(scaled, a_border[...], NN, preferred_element_type=F32).astype(BF16)
        for lane_at in range(lanes):
            rsend[t, lane_at, :, own : own + 128] = border[:, lane_at * 128 : (lane_at + 1) * 128]
            rsend[t, lane_at, :, own + 128 : own + 256] = coeff

        def spread(peer):
            return lax.dot_general(scaled, a_own[peer], NN, preferred_element_type=F32).astype(BF16)

        def push(d):
            peer = row_peer(d)
            rsend[t, peer, :, 0:own] = spread(peer)
            row_copy((r_s, r_r), t, d, rsend.at[t, peer], rbuf.at[t, w]).start()

        each(1, lanes, push)
        rbuf[t, w, :, 0:own] = spread(w)
        rbuf[t, w, :, own : own + 256] = rsend[t, w, :, own : own + 256]

    def adjoint_merge(t):
        low = own + 128 if t == 0 else 0
        part = pl.ds(low, own + 256 - low)
        each(
            1,
            lanes,
            lambda d: arrive(r_r, t, row_peer(d), rbuf.at[t, row_peer(d), :, part]),
        )
        summed = rbuf[t, 0, :, part].astype(F32)
        for lane_at in range(1, lanes):
            summed = summed + rbuf[t, lane_at, :, part].astype(F32)
        coeff = fold(summed[:, own + 128 - low :], rank)
        coeff_low = coeff - round_trip(coeff)
        if t == 0:
            border = border_low = jnp.zeros((batch, 128), F32)
        else:
            border = summed[:, own : own + 128]
            border_low = pltpu.roll(border - round_trip(border), bsrc, 1)
        for s in range(groups):
            tile = jnp.where(
                is_border(s),
                border,
                jnp.where(is_low_border(s), border_low, jnp.where(is_high(s), coeff, coeff_low)),
            )
            azsend[t, s] = tile.astype(BF16)
        each(
            1,
            groups,
            lambda d: region_copy(
                (az_s, az_r), t, d, azsend.at[t, region_peer(d)], azbuf.at[t, g]
            ).start(),
        )
        azbuf[t, g] = azsend[t, g]
        return None if t == 0 else summed[:, :own]

    def adjoint_finish(t, through):
        each(1, groups, lambda d: arrive(az_r, t, region_peer(d), azbuf.at[t, region_peer(d)]))
        mine = is_sum(g)
        coeff = jnp.zeros((batch, 128), F32)
        for s in range(groups):
            coeff = coeff + jnp.where(mine, azbuf[t, s].astype(F32), 0.0)
        coeff = round_trip(fold(coeff, rank))
        coef_sv[t * batch : (t + 1) * batch, :] = coeff
        if t == 0:
            return None
        home = offset(g) < 2 * bsrc
        tiles = []
        for s in range(groups):
            rest = jnp.where(is_high(g), coeff, 0.0) if s == 0 else jnp.zeros_like(coeff)
            tiles.append(jnp.where(home, azbuf[t, s].astype(F32), rest).astype(BF16))
        return through + lax.dot_general(
            jnp.concatenate(tiles, axis=1), pick[...], NT, preferred_element_type=F32
        )

    def adjoint_step(t, adjoint, total):
        rates = rates_sv[t]
        return (1.0 - LEAK) * adjoint + (1.0 - rates * rates) * polarity * total

    pl.semaphore_wait(barrier, lanes + groups - 2)

    last = STEPS - 1
    state = state_ref[...]
    forward_send(0, state)
    forward_merge(0)
    load_own.wait()
    load_border.wait()
    state = forward_finish(0, state)

    forward_send(1, state)
    forward_merge(1)
    adjoint_send(last, cot_ref[...])
    state = forward_finish(1, state)

    forward_send(2, state)
    through = adjoint_merge(last)
    forward_merge(2)
    adj_sv[...] = adjoint_finish(last, through)
    state = forward_finish(2, state)

    rates_sv[last] = jnp.tanh(state)
    state_sv[...] = state
    adjoint = adjoint_step(last, cot_ref[...], adj_sv[...])
    adjoint_send(2, adjoint)
    through = adjoint_merge(2)
    forward_send(last, state_sv[...])
    adjoint = adjoint_step(2, adjoint, adjoint_finish(2, through))
    forward_merge(last)
    adjoint_send(1, adjoint)
    final_ref[...] = forward_finish(last, state_sv[...])
    through = adjoint_merge(1)
    adjoint = adjoint_step(1, adjoint, adjoint_finish(1, through))
    adjoint_send(0, adjoint)
    lat = lat_sv[...].T[:rank].astype(BF16)
    gu_ref[...] = lax.dot_general(lat, scaled_sv[...], NN, preferred_element_type=F32)
    adjoint_merge(0)
    adjoint_finish(0, None)
    coef = coef_sv[...].T[:rank].astype(BF16)
    signed_all = jnp.concatenate([signed_sv[t] for t in range(STEPS)], axis=0)
    gv_ref[...] = lax.dot_general(coef, signed_all, NN, preferred_element_type=F32)

    for t in range(STEPS):
        each(
            1,
            groups,
            lambda d: region_copy(
                (z_s, z_r), t, d, zsend.at[t, region_peer(d)], zbuf.at[t, g]
            ).wait_send(),
        )
        each(
            1,
            groups,
            lambda d: region_copy(
                (az_s, az_r), t, d, azsend.at[t, region_peer(d)], azbuf.at[t, g]
            ).wait_send(),
        )

        def drain(d):
            row_copy((ext_s, ext_r), t, d, ext.at[t, w], ext.at[t, w]).wait_send()
            row_copy((b_s, b_r), t, d, bbuf.at[t, w], bbuf.at[t, w]).wait_send()
            if t == 0:
                part = pl.ds(own + 128, 128)
                row_copy(
                    (r_s, r_r), t, d, rbuf.at[t, w, :, part], rbuf.at[t, w, :, part]
                ).wait_send()
            else:
                row_copy((r_s, r_r), t, d, rsend.at[t, row_peer(d)], rbuf.at[t, w]).wait_send()

        each(1, lanes, drain)


def local(
    state0,
    drive,
    cotangent,
    excitatory,
    tile_vals,
    tile_cols,
    tile_count,
    boundary_rows,
    u_factor,
    v_factor,
):
    lanes = lax.axis_size("row")
    groups, bsrc = boundary_rows.shape[2:]
    batch, own = state0.shape
    rank = u_factor.shape[0]
    a_own, a_border = densify(tile_vals, tile_cols, tile_count, lanes, own)
    rows = boundary_rows.reshape(groups, bsrc)
    vmem = pl.BlockSpec(memory_space=pltpu.VMEM)
    hbm = pl.BlockSpec(memory_space=pl.ANY)
    dma = pltpu.SemaphoreType.DMA
    out = jax.ShapeDtypeStruct((batch, own), F32)
    grad = jax.ShapeDtypeStruct((rank, own), F32)
    return pl.pallas_call(
        functools.partial(step_kernel, groups, lanes, bsrc),
        out_shape=(out, grad, grad),
        in_specs=[vmem, vmem, vmem, vmem, hbm, hbm, vmem, vmem, vmem],
        out_specs=(vmem, vmem, vmem),
        scratch_shapes=[
            pltpu.VMEM((lanes, own, own), BF16),
            pltpu.VMEM((own, lanes * 128), BF16),
            pltpu.VMEM((own, groups * 128), BF16),
            pltpu.VMEM((STEPS, lanes, batch, own), BF16),
            pltpu.VMEM((STEPS, groups, batch, 128), BF16),
            pltpu.VMEM((STEPS, groups, batch, 128), BF16),
            pltpu.VMEM((STEPS, lanes, batch, 256), BF16),
            pltpu.VMEM((STEPS, lanes, batch, own + 256), BF16),
            pltpu.VMEM((STEPS, lanes, batch, own + 256), BF16),
            pltpu.VMEM((STEPS, groups, batch, 128), BF16),
            pltpu.VMEM((STEPS, groups, batch, 128), BF16),
            pltpu.VMEM((STEPS, batch, own), F32),
            pltpu.VMEM((STEPS, batch, own), BF16),
            pltpu.VMEM((STEPS * batch, own), BF16),
            pltpu.VMEM((STEPS * batch, 128), F32),
            pltpu.VMEM((STEPS * batch, 128), F32),
            pltpu.VMEM((batch, own), F32),
            pltpu.VMEM((batch, own), F32),
            dma((2,)),
            dma((STEPS, lanes)),
            dma((STEPS, lanes)),
            dma((STEPS, groups)),
            dma((STEPS, groups)),
            dma((STEPS, lanes)),
            dma((STEPS, lanes)),
            dma((STEPS, lanes)),
            dma((STEPS, lanes)),
            dma((STEPS, groups)),
            dma((STEPS, groups)),
        ],
        compiler_params=pltpu.CompilerParams(
            collective_id=0, has_side_effects=True, vmem_limit_bytes=60 * 1024 * 1024
        ),
    )(
        state0,
        drive,
        cotangent,
        excitatory.reshape(1, own),
        a_own,
        a_border,
        rows,
        u_factor,
        v_factor,
    )


def solution(mesh):
    return jax.shard_map(
        local,
        mesh=mesh,
        in_specs=(
            P(None, ("region", "row")),
            P(None, ("region", "row")),
            P(None, ("region", "row")),
            P(("region", "row")),
            P(("region", "row"), None, None, None),
            P(("region", "row"), None),
            P(("region", "row")),
            P("region", "row", None, None),
            P(None, ("region", "row")),
            P(None, ("region", "row")),
        ),
        out_specs=(
            P(None, ("region", "row")),
            P(None, ("region", "row")),
            P(None, ("region", "row")),
        ),
        check_vma=False,
    )
```

```python
import functools

import jax
import jax.numpy as jnp
from jax import lax
from jax.experimental import pallas as pl
from jax.experimental.pallas import tpu as pltpu
from jax.sharding import PartitionSpec as P

STEPS = 4
LEAK = 0.5
F32 = jnp.float32
BF16 = jnp.bfloat16
MESH = pl.DeviceIdType.MESH
NT = (((1,), (1,)), ((), ()))
NN = (((1,), (0,)), ((), ()))


def dense_kernel(lanes, per_lane, cols_ref, count_ref, vals_ref, own_ref, border_ref, acc):
    q = pl.program_id(0)
    own_tiles = per_lane - 1
    acc[...] = jnp.zeros_like(acc)

    def add(j, carry):
        c = cols_ref[q, j]
        acc[c] = acc[c] + vals_ref[0, j].astype(F32)
        return carry

    lax.fori_loop(0, count_ref[q], add, 0)
    for lane in range(lanes):
        for i in range(own_tiles):
            own_ref[lane, :, i * 128 : (i + 1) * 128] = acc[lane * per_lane + i].astype(BF16)
        border_ref[:, lane * 128 : (lane + 1) * 128] = acc[lane * per_lane + own_tiles].astype(BF16)


def densify(tile_vals, tile_cols, tile_count, lanes, own_rows):
    row_tiles, kmax = tile_vals.shape[:2]
    per_lane = own_rows // 128 + 1
    return pl.pallas_call(
        functools.partial(dense_kernel, lanes, per_lane),
        out_shape=(
            jax.ShapeDtypeStruct((lanes, own_rows, own_rows), BF16),
            jax.ShapeDtypeStruct((own_rows, lanes * 128), BF16),
        ),
        grid_spec=pltpu.PrefetchScalarGridSpec(
            num_scalar_prefetch=2,
            grid=(row_tiles,),
            in_specs=[pl.BlockSpec((1, kmax, 128, 128), lambda q, *_: (q, 0, 0, 0))],
            out_specs=[
                pl.BlockSpec((lanes, 128, own_rows), lambda q, *_: (0, q, 0)),
                pl.BlockSpec((128, lanes * 128), lambda q, *_: (q, 0)),
            ],
            scratch_shapes=[pltpu.VMEM((lanes * per_lane, 128, 128), F32)],
        ),
        compiler_params=pltpu.CompilerParams(vmem_limit_bytes=48 * 1024 * 1024),
    )(tile_cols, tile_count, tile_vals)


def fold(x, rank):
    shift = 64
    while shift >= rank:
        x = x + pltpu.roll(x, shift, 1)
        shift //= 2
    return x


def round_trip(x):
    return x.astype(BF16).astype(F32)


def step_kernel(
    groups,
    lanes,
    bsrc,
    state_ref,
    drive_ref,
    cot_ref,
    exc_ref,
    own_hbm,
    border_hbm,
    rows_ref,
    u_ref,
    v_ref,
    final_ref,
    gu_ref,
    gv_ref,
    a_own,
    a_border,
    pick,
    ext,
    zsend,
    zbuf,
    bbuf,
    rsend,
    rbuf,
    azsend,
    azbuf,
    rates_sv,
    signed_sv,
    scaled_sv,
    lat_sv,
    coef_sv,
    adj_sv,
    state_sv,
    load_sem,
    ext_s,
    ext_r,
    z_s,
    z_r,
    b_s,
    b_r,
    r_s,
    r_r,
    az_s,
    az_r,
):
    g = lax.axis_index("region")
    w = lax.axis_index("row")
    batch, own = state_ref.shape
    rank = u_ref.shape[0]

    load_own = pltpu.make_async_copy(own_hbm, a_own, load_sem.at[0])
    load_border = pltpu.make_async_copy(border_hbm, a_border, load_sem.at[1])
    load_own.start()
    load_border.start()

    def row_peer(d):
        return lax.rem(w + d, lanes)

    def region_peer(d):
        return lax.rem(g + d, groups)

    barrier = pltpu.get_barrier_semaphore()

    def greet_row(d, carry):
        pl.semaphore_signal(barrier, inc=1, device_id=(g, row_peer(d)), device_id_type=MESH)
        return carry

    def greet_region(d, carry):
        pl.semaphore_signal(barrier, inc=1, device_id=(region_peer(d), w), device_id_type=MESH)
        return carry

    lax.fori_loop(1, lanes, greet_row, 0)
    lax.fori_loop(1, groups, greet_region, 0)

    lane = lax.broadcasted_iota(jnp.int32, (batch, 128), 1)

    def offset(s):
        return lax.rem(lane + (128 * bsrc - bsrc * s), 128)

    def is_border(s):
        return offset(s) < bsrc

    def is_low_border(s):
        return (offset(s) >= bsrc) & (offset(s) < 2 * bsrc)

    def is_high(s):
        return (offset(s) >= 2 * bsrc) & (offset(s) < 2 * bsrc + rank)

    def is_low(s):
        return (offset(s) >= 2 * bsrc + rank) & (offset(s) < 2 * bsrc + 2 * rank)

    def is_sum(s):
        return is_high(s) | is_low(s)

    def sum_tile(x):
        high = round_trip(x)
        return jnp.where(lane < rank, x, jnp.where(lane < 2 * rank, x - high, 0.0)).astype(BF16)

    polarity = (2 * exc_ref[...] - 1).astype(F32)
    u_all = jnp.concatenate([u_ref[...]] * (128 // rank), axis=0)
    v_cols = jnp.concatenate([v_ref[...].astype(F32)] * (128 // rank), axis=0).T
    sub = lax.broadcasted_iota(jnp.int32, (own, 128), 0)
    own_lane = lax.rem(
        lax.broadcasted_iota(jnp.int32, (own, 128), 1) + (128 * bsrc - bsrc * g), 128
    )
    rows = jnp.concatenate([rows_ref[...]] * (128 // bsrc), axis=1)
    for s in range(groups):
        hot = jnp.where(sub == rows[s : s + 1, :], 1.0, 0.0)
        pick[:, s * 128 : (s + 1) * 128] = jnp.where(own_lane < 2 * bsrc, hot, v_cols).astype(BF16)

    half = lanes // 2
    peer_groups = (range(1, half), range(half, lanes))

    def row_copy(kind, t, d, src, dst):
        send, recv = kind
        return pltpu.make_async_remote_copy(
            src_ref=src,
            dst_ref=dst,
            send_sem=send.at[t, d],
            recv_sem=recv.at[t, w],
            device_id=(g, row_peer(d)),
            device_id_type=MESH,
        )

    def region_copy(kind, t, d, src, dst):
        send, recv = kind
        return pltpu.make_async_remote_copy(
            src_ref=src,
            dst_ref=dst,
            send_sem=send.at[t, d],
            recv_sem=recv.at[t, g],
            device_id=(region_peer(d), w),
            device_id_type=MESH,
        )

    def arrive(recv, t, source, ref):
        pltpu.make_async_copy(ref, ref, recv.at[t, source]).wait()

    def each(low, high, body):
        def step(d, carry):
            body(d)
            return carry

        lax.fori_loop(low, high, step, 0)

    def forward_send(t, state):
        rates = jnp.tanh(state)
        signed = (polarity * rates).astype(BF16)
        rates_sv[t] = rates
        signed_sv[t] = signed
        message = lax.dot_general(signed, pick[...], NN, preferred_element_type=F32)
        mine_low = is_low(g)
        for s in range(groups):
            tile = message[:, s * 128 : (s + 1) * 128]
            zsend[t, s] = jnp.where(mine_low, tile - round_trip(tile), tile).astype(BF16)
        each(
            1,
            groups,
            lambda d: region_copy(
                (z_s, z_r), t, d, zsend.at[t, region_peer(d)], zbuf.at[t, g]
            ).start(),
        )
        ext[t, w] = signed
        each(
            1,
            lanes,
            lambda d: row_copy((ext_s, ext_r), t, d, ext.at[t, w], ext.at[t, w]).start(),
        )
        zbuf[t, g] = zsend[t, g]

    def forward_merge(t):
        each(1, groups, lambda d: arrive(z_r, t, region_peer(d), zbuf.at[t, region_peer(d)]))
        border = jnp.zeros((batch, 128), F32)
        latent = jnp.zeros((batch, 128), F32)
        for s in range(groups):
            tile = zbuf[t, s].astype(F32)
            border = jnp.where(is_border(s), tile, border)
            latent = latent + jnp.where(is_sum(s), tile, 0.0)
        bbuf[t, w, :, 0:128] = border.astype(BF16)
        bbuf[t, w, :, 128:256] = sum_tile(fold(latent, rank))
        each(
            1,
            lanes,
            lambda d: row_copy((b_s, b_r), t, d, bbuf.at[t, w], bbuf.at[t, w]).start(),
        )

    def forward_finish(t, state):
        def gather(d, total):
            peer = row_peer(d)
            arrive(ext_r, t, peer, ext.at[t, peer])
            return total + lax.dot_general(
                ext[t, peer], a_own[peer], NT, preferred_element_type=F32
            )

        total = lax.dot_general(ext[t, w], a_own[w], NT, preferred_element_type=F32)
        if lanes <= 8:
            for batch_of in peer_groups:
                for d in batch_of:
                    arrive(ext_r, t, row_peer(d), ext.at[t, row_peer(d)])
                for d in batch_of:
                    total = total + lax.dot_general(
                        ext[t, row_peer(d)], a_own[row_peer(d)], NT, preferred_element_type=F32
                    )
        else:
            total = lax.fori_loop(1, lanes, gather, total)
        each(1, lanes, lambda d: arrive(b_r, t, row_peer(d), bbuf.at[t, row_peer(d)]))
        latent = jnp.zeros((batch, 128), F32)
        tiles = []
        for lane_at in range(lanes):
            tiles.append(bbuf[t, lane_at, :, 0:128])
            latent = latent + bbuf[t, lane_at, :, 128:256].astype(F32)
        total = total + lax.dot_general(
            jnp.concatenate(tiles, axis=1), a_border[...], NT, preferred_element_type=F32
        )
        latent = round_trip(fold(latent, rank))
        lat_sv[t * batch : (t + 1) * batch, :] = latent
        total = total + lax.dot_general(
            latent[:, :rank].astype(BF16), u_ref[...], NN, preferred_element_type=F32
        )
        return state + LEAK * (-state + total + drive_ref[...].astype(F32))

    def adjoint_send(t, adjoint):
        scaled = (LEAK * adjoint).astype(BF16)
        scaled_sv[t * batch : (t + 1) * batch, :] = scaled
        coeff = sum_tile(lax.dot_general(scaled, u_all, NT, preferred_element_type=F32))
        if t == 0:
            rbuf[t, w, :, own + 128 : own + 256] = coeff
            part = pl.ds(own + 128, 128)
            each(
                1,
                lanes,
                lambda d: row_copy(
                    (r_s, r_r), t, d, rbuf.at[t, w, :, part], rbuf.at[t, w, :, part]
                ).start(),
            )
            return
        border = lax.dot_general(scaled, a_border[...], NN, preferred_element_type=F32).astype(BF16)
        for lane_at in range(lanes):
            rsend[t, lane_at, :, own : own + 128] = border[:, lane_at * 128 : (lane_at + 1) * 128]
            rsend[t, lane_at, :, own + 128 : own + 256] = coeff

        def spread(peer):
            return lax.dot_general(scaled, a_own[peer], NN, preferred_element_type=F32).astype(BF16)

        def push(d):
            peer = row_peer(d)
            rsend[t, peer, :, 0:own] = spread(peer)
            row_copy((r_s, r_r), t, d, rsend.at[t, peer], rbuf.at[t, w]).start()

        if lanes <= 8:
            for batch_of in peer_groups:
                for d in batch_of:
                    rsend[t, row_peer(d), :, 0:own] = spread(row_peer(d))
                for d in batch_of:
                    peer = row_peer(d)
                    row_copy((r_s, r_r), t, d, rsend.at[t, peer], rbuf.at[t, w]).start()
        else:
            each(1, lanes, push)
        rbuf[t, w, :, 0:own] = spread(w)
        rbuf[t, w, :, own : own + 256] = rsend[t, w, :, own : own + 256]

    def adjoint_merge(t):
        low = own + 128 if t == 0 else 0
        part = pl.ds(low, own + 256 - low)
        each(
            1,
            lanes,
            lambda d: arrive(r_r, t, row_peer(d), rbuf.at[t, row_peer(d), :, part]),
        )
        summed = rbuf[t, 0, :, part].astype(F32)
        for lane_at in range(1, lanes):
            summed = summed + rbuf[t, lane_at, :, part].astype(F32)
        coeff = fold(summed[:, own + 128 - low :], rank)
        coeff_low = coeff - round_trip(coeff)
        if t == 0:
            border = border_low = jnp.zeros((batch, 128), F32)
        else:
            border = summed[:, own : own + 128]
            border_low = pltpu.roll(border - round_trip(border), bsrc, 1)
        for s in range(groups):
            tile = jnp.where(
                is_border(s),
                border,
                jnp.where(is_low_border(s), border_low, jnp.where(is_high(s), coeff, coeff_low)),
            )
            azsend[t, s] = tile.astype(BF16)
        each(
            1,
            groups,
            lambda d: region_copy(
                (az_s, az_r), t, d, azsend.at[t, region_peer(d)], azbuf.at[t, g]
            ).start(),
        )
        azbuf[t, g] = azsend[t, g]
        return None if t == 0 else summed[:, :own]

    def adjoint_finish(t, through):
        each(1, groups, lambda d: arrive(az_r, t, region_peer(d), azbuf.at[t, region_peer(d)]))
        mine = is_sum(g)
        coeff = jnp.zeros((batch, 128), F32)
        for s in range(groups):
            coeff = coeff + jnp.where(mine, azbuf[t, s].astype(F32), 0.0)
        coeff = round_trip(fold(coeff, rank))
        coef_sv[t * batch : (t + 1) * batch, :] = coeff
        if t == 0:
            return None
        home = offset(g) < 2 * bsrc
        tiles = []
        for s in range(groups):
            rest = jnp.where(is_high(g), coeff, 0.0) if s == 0 else jnp.zeros_like(coeff)
            tiles.append(jnp.where(home, azbuf[t, s].astype(F32), rest).astype(BF16))
        return through + lax.dot_general(
            jnp.concatenate(tiles, axis=1), pick[...], NT, preferred_element_type=F32
        )

    def adjoint_step(t, adjoint, total):
        rates = rates_sv[t]
        return (1.0 - LEAK) * adjoint + (1.0 - rates * rates) * polarity * total

    pl.semaphore_wait(barrier, lanes + groups - 2)

    last = STEPS - 1
    state = state_ref[...]
    forward_send(0, state)
    forward_merge(0)
    load_own.wait()
    load_border.wait()
    state = forward_finish(0, state)

    forward_send(1, state)
    forward_merge(1)
    adjoint_send(last, cot_ref[...])
    state = forward_finish(1, state)

    forward_send(2, state)
    through = adjoint_merge(last)
    forward_merge(2)
    adj_sv[...] = adjoint_finish(last, through)
    state = forward_finish(2, state)

    rates_sv[last] = jnp.tanh(state)
    state_sv[...] = state
    adjoint = adjoint_step(last, cot_ref[...], adj_sv[...])
    adjoint_send(2, adjoint)
    through = adjoint_merge(2)
    forward_send(last, state_sv[...])
    adjoint = adjoint_step(2, adjoint, adjoint_finish(2, through))
    forward_merge(last)
    adjoint_send(1, adjoint)
    final_ref[...] = forward_finish(last, state_sv[...])
    through = adjoint_merge(1)
    adjoint = adjoint_step(1, adjoint, adjoint_finish(1, through))
    adjoint_send(0, adjoint)
    lat = lat_sv[...].T[:rank].astype(BF16)
    gu_ref[...] = lax.dot_general(lat, scaled_sv[...], NN, preferred_element_type=F32)
    adjoint_merge(0)
    adjoint_finish(0, None)
    coef = coef_sv[...].T[:rank].astype(BF16)
    signed_all = jnp.concatenate([signed_sv[t] for t in range(STEPS)], axis=0)
    gv_ref[...] = lax.dot_general(coef, signed_all, NN, preferred_element_type=F32)

    for t in range(STEPS):
        each(
            1,
            groups,
            lambda d: region_copy(
                (z_s, z_r), t, d, zsend.at[t, region_peer(d)], zbuf.at[t, g]
            ).wait_send(),
        )
        each(
            1,
            groups,
            lambda d: region_copy(
                (az_s, az_r), t, d, azsend.at[t, region_peer(d)], azbuf.at[t, g]
            ).wait_send(),
        )

        def drain(d):
            row_copy((ext_s, ext_r), t, d, ext.at[t, w], ext.at[t, w]).wait_send()
            row_copy((b_s, b_r), t, d, bbuf.at[t, w], bbuf.at[t, w]).wait_send()
            if t == 0:
                part = pl.ds(own + 128, 128)
                row_copy(
                    (r_s, r_r), t, d, rbuf.at[t, w, :, part], rbuf.at[t, w, :, part]
                ).wait_send()
            else:
                row_copy((r_s, r_r), t, d, rsend.at[t, row_peer(d)], rbuf.at[t, w]).wait_send()

        each(1, lanes, drain)


def local(
    state0,
    drive,
    cotangent,
    excitatory,
    tile_vals,
    tile_cols,
    tile_count,
    boundary_rows,
    u_factor,
    v_factor,
):
    lanes = lax.axis_size("row")
    groups, bsrc = boundary_rows.shape[2:]
    batch, own = state0.shape
    rank = u_factor.shape[0]
    a_own, a_border = densify(tile_vals, tile_cols, tile_count, lanes, own)
    rows = boundary_rows.reshape(groups, bsrc)
    vmem = pl.BlockSpec(memory_space=pltpu.VMEM)
    hbm = pl.BlockSpec(memory_space=pl.ANY)
    dma = pltpu.SemaphoreType.DMA
    out = jax.ShapeDtypeStruct((batch, own), F32)
    grad = jax.ShapeDtypeStruct((rank, own), F32)
    return pl.pallas_call(
        functools.partial(step_kernel, groups, lanes, bsrc),
        out_shape=(out, grad, grad),
        in_specs=[vmem, vmem, vmem, vmem, hbm, hbm, vmem, vmem, vmem],
        out_specs=(vmem, vmem, vmem),
        scratch_shapes=[
            pltpu.VMEM((lanes, own, own), BF16),
            pltpu.VMEM((own, lanes * 128), BF16),
            pltpu.VMEM((own, groups * 128), BF16),
            pltpu.VMEM((STEPS, lanes, batch, own), BF16),
            pltpu.VMEM((STEPS, groups, batch, 128), BF16),
            pltpu.VMEM((STEPS, groups, batch, 128), BF16),
            pltpu.VMEM((STEPS, lanes, batch, 256), BF16),
            pltpu.VMEM((STEPS, lanes, batch, own + 256), BF16),
            pltpu.VMEM((STEPS, lanes, batch, own + 256), BF16),
            pltpu.VMEM((STEPS, groups, batch, 128), BF16),
            pltpu.VMEM((STEPS, groups, batch, 128), BF16),
            pltpu.VMEM((STEPS, batch, own), F32),
            pltpu.VMEM((STEPS, batch, own), BF16),
            pltpu.VMEM((STEPS * batch, own), BF16),
            pltpu.VMEM((STEPS * batch, 128), F32),
            pltpu.VMEM((STEPS * batch, 128), F32),
            pltpu.VMEM((batch, own), F32),
            pltpu.VMEM((batch, own), F32),
            dma((2,)),
            dma((STEPS, lanes)),
            dma((STEPS, lanes)),
            dma((STEPS, groups)),
            dma((STEPS, groups)),
            dma((STEPS, lanes)),
            dma((STEPS, lanes)),
            dma((STEPS, lanes)),
            dma((STEPS, lanes)),
            dma((STEPS, groups)),
            dma((STEPS, groups)),
        ],
        compiler_params=pltpu.CompilerParams(
            collective_id=0, has_side_effects=True, vmem_limit_bytes=60 * 1024 * 1024
        ),
    )(
        state0,
        drive,
        cotangent,
        excitatory.reshape(1, own),
        a_own,
        a_border,
        rows,
        u_factor,
        v_factor,
    )


def solution(mesh):
    return jax.shard_map(
        local,
        mesh=mesh,
        in_specs=(
            P(None, ("region", "row")),
            P(None, ("region", "row")),
            P(None, ("region", "row")),
            P(("region", "row")),
            P(("region", "row"), None, None, None),
            P(("region", "row"), None),
            P(("region", "row")),
            P("region", "row", None, None),
            P(None, ("region", "row")),
            P(None, ("region", "row")),
        ),
        out_specs=(
            P(None, ("region", "row")),
            P(None, ("region", "row")),
            P(None, ("region", "row")),
        ),
        check_vma=False,
    )
```
